32 devices in a mesh: dp: 8 (over z, x), tensor: 4 (over y, core).
Axes of the slice: x: 2, y: 2, z: 4, core: 2. Of those that a mesh axis runs over, the one named last changes fastest.
Arguments:
- gate_grads: bfloat16 [8, 256, 8192], P('dp', 'tensor'), may hold values from -6 to 6
- up_grads: bfloat16 [8, 256, 8192], P('dp', 'tensor'), may hold values from -6 to 6
- gate_errors: bfloat16 [8, 256, 8192], P('dp', 'tensor'), may hold values from -3 to 3
- up_errors: bfloat16 [8, 256, 8192], P('dp', 'tensor'), may hold values from -3 to 3
- gate_start: float32 [8192, 32], replicated, may hold values from -6 to 6
- up_start: float32 [8192, 32], replicated, may hold values from -6 to 6
Outputs:
- gate_mean: bfloat16 [256, 8192], P('tensor')
- up_mean: bfloat16 [256, 8192], P('tensor')
- gate_new_errors: bfloat16 [8, 256, 8192], P('dp', 'tensor')
- up_new_errors: bfloat16 [8, 256, 8192], P('dp', 'tensor')
The draws below stay inside these ranges and needn't reach their ends.
All inputs are finite; a program needn't handle non-finite values.
Results may differ from the reference program's by a relative error of at most 0.0015.
Values sent between devices are 32-bit elements; how exact they have to be, the bound alone decides.
A program may use at most 64 MiB of HBM per device.

```python
import jax
import jax.numpy as jnp
from jax import lax

COLS = 8192
RANK = 32
BUCKET = 256
REPLICAS = 8


def block_levels(own_key, extent, split, smallest, top_value):
    loudness, own = 1.0, jax.random.fold_in(own_key, 6)
    for dim, shards_of in split:
        draws = jnp.exp(jax.random.uniform(jax.random.fold_in(own, dim), (shards_of,), jnp.float32, smallest / len(split), top_value / len(split)))
        loudness = loudness * jnp.repeat(draws, extent[dim] // shards_of).reshape([-1 if axis == dim else 1 for axis in range(len(extent))])
    return loudness


def gaussian(rng, extent, spread, most, shards=(), held_as=jnp.bfloat16):
    array = jax.random.normal(rng, extent, jnp.float32) * spread
    if len(shards) > 0:
        array = block_levels(rng, extent, shards, -0.22, 0.18) * array
    return jnp.clip(array, min=-most, max=most).astype(held_as)


def setup_inputs(seed: int = 0) -> dict:
    streams_of = jax.random.split(jax.random.key(seed), 7)
    return {
        "gate_grads": gaussian(streams_of[0], (REPLICAS, BUCKET, COLS), 1.0, 6.0, ((0, 8), (1, 4))),
        "up_grads": gaussian(streams_of[1], (REPLICAS, BUCKET, COLS), 1.0, 6.0, ((0, 8), (1, 4))),
        "gate_errors": gaussian(streams_of[2], (REPLICAS, BUCKET, COLS), 0.5, 3.0, ((0, 8), (1, 4))),
        "up_errors": gaussian(streams_of[3], (REPLICAS, BUCKET, COLS), 0.5, 3.0, ((0, 8), (1, 4))),
        "gate_start": gaussian(streams_of[4], (COLS, RANK), 1.0, 6.0, (), jnp.float32),
        "up_start": gaussian(streams_of[5], (COLS, RANK), 1.0, 6.0, (), jnp.float32),
    }


def compress(grads, errors, start):
    full = grads.astype(jnp.float32) + errors.astype(jnp.float32)
    left = jnp.einsum('knc,cr->nr', full, start, precision=lax.Precision.HIGHEST) / REPLICAS
    gram = jnp.dot(left.T, left, precision=lax.Precision.HIGHEST)
    lower = jnp.linalg.cholesky(gram)
    basis = lax.linalg.triangular_solve(lower, left, left_side=False, lower=True, transpose_a=True)
    right = jnp.einsum('knc,nr->cr', full, basis, precision=lax.Precision.HIGHEST) / REPLICAS
    approx = jnp.dot(basis, right.T, precision=lax.Precision.HIGHEST)
    return (approx.astype(jnp.bfloat16), (full - approx[None]).astype(jnp.bfloat16))

def reference(gate_grads, up_grads, gate_errors, up_errors, gate_start, up_start):
    gate_mean, gate_new = compress(gate_grads, gate_errors, gate_start)
    up_mean, up_new = compress(up_grads, up_errors, up_start)
    return (gate_mean, up_mean, gate_new, up_new)
```

```python
import functools

import jax
import jax.numpy as jnp
from jax import lax
from jax.experimental import pallas as pl
from jax.experimental.pallas import tpu as pltpu
from jax.sharding import PartitionSpec as P

F32 = jnp.float32
BF16 = jnp.bfloat16
HIGHEST = lax.Precision.HIGHEST
LOADS = 4
CHUNKS = 2
BLOCK = 512


def split3(x):
    a = x.astype(BF16)
    r = x - a.astype(F32)
    b = r.astype(BF16)
    c = (r - b.astype(F32)).astype(BF16)
    return a, b, c


def spd_inverse(a):
    n = a.shape[0]
    rows = lax.broadcasted_iota(jnp.int32, (n, n), 0)
    cols = lax.broadcasted_iota(jnp.int32, (n, n), 1)
    for k in range(n):
        row = a[k:k + 1, :]
        col = a[:, k:k + 1]
        inv = 1.0 / row[:, k:k + 1]
        scaled = row * inv
        new = jnp.where(cols == k, -col * inv, a - col * scaled)
        a = jnp.where(rows == k, jnp.where(cols == k, inv, scaled), new)
    return a


class Plan:
    def __init__(self, ndp, nt, cols, rank):
        self.core = ("tensor", 1, 2)
        self.y = ("tensor", 2, nt // 2)
        self.x = ("dp", 1, 2)
        self.z = ("dp", 2, ndp // 2)
        self.orders = ((self.core, self.x, self.y, self.z), (self.core, self.y, self.x, self.z))
        self.tiles = (rank // 8) * (cols // 128)
        self.half = self.tiles // 2
        shards = (ndp * nt) // 2
        self.chunks = max(1, min(CHUNKS, self.half // shards))
        assert self.half % (shards * self.chunks) == 0
        self.sizes = []
        for order in self.orders:
            t = [self.half // self.chunks]
            for _, _, n in order[1:]:
                t.append(t[-1] // n)
            self.sizes.append(t)
        self.stages = 4
        self.copies = sum(n - 1 for _, _, n in self.orders[0])


def kernel(plan, ndp, nt, rank, *refs):
    grads, errors, starts = refs[0:2], refs[2:4], refs[4:6]
    w_out, c_out = refs[6:8]
    (ge, st, pbuf, gbuf, part, full, cbuf) = refs[8:15]
    k = 15
    recv = (refs[k:k + 4], refs[k + 4:k + 8])
    acc = (refs[k + 8:k + 11], refs[k + 11:k + 14])
    k += 14
    (load_sem, p_send, p_recv, g_send, g_recv, rs_send, rs_recv, ag_send, ag_recv, out_sem) = refs[k:]

    idx = {"dp": lax.axis_index("dp"), "tensor": lax.axis_index("tensor")}
    size = {"dp": ndp, "tensor": nt}

    def device(axis, i):
        return (i, idx["tensor"]) if axis == "dp" else (idx["dp"], i)

    barrier = pltpu.get_barrier_semaphore()
    for axis in ("dp", "tensor"):
        for o in range(1, size[axis]):
            pl.semaphore_signal(barrier, inc=1, device_id=device(axis, lax.rem(idx[axis] + o, size[axis])),
                                device_id_type=pl.DeviceIdType.MESH)

    n_local, cols = grads[0].shape
    width = cols // LOADS
    loads = {}
    for p in range(2):
        for b in range(LOADS):
            span = pl.ds(b * width, width)
            trio = (
                (starts[p].at[:, span], st.at[p, :, span]),
                (grads[p].at[:, span], ge.at[p, pl.ds(0, n_local), span]),
                (errors[p].at[:, span], ge.at[p, pl.ds(n_local, n_local), span]),
            )
            for m, (src, dst) in enumerate(trio):
                copy = pltpu.make_async_copy(src, dst, load_sem.at[p, b, m])
                copy.start()
                loads[p, b, m] = copy

    terms = []
    for p in range(2):
        total = jnp.zeros((3 * rank, 2 * n_local), F32)
        for b in range(LOADS):
            for m in range(3):
                loads[p, b, m].wait()
            s3 = jnp.concatenate(split3(st[p, :, b * width:(b + 1) * width]), axis=0)
            total += lax.dot_general(s3, ge[p, :, b * width:(b + 1) * width], (((1,), (1,)), ((), ())),
                                     preferred_element_type=F32)
        t = (total[2 * rank:] + total[rank:2 * rank]) + total[:rank]
        terms.append(t[:, :n_local] + t[:, n_local:])
    pbuf[0] = jnp.concatenate(terms, axis=1)

    pl.semaphore_wait(barrier, ndp + nt - 2)
    sends = []

    def exchange(buf, axis, send_sem, recv_sem):
        n = size[axis]
        copies = []
        for o in range(1, n):
            copy = pltpu.make_async_remote_copy(
                src_ref=buf.at[0], dst_ref=buf.at[o], send_sem=send_sem.at[o - 1], recv_sem=recv_sem.at[o - 1],
                device_id=device(axis, lax.rem(idx[axis] + o, n)), device_id_type=pl.DeviceIdType.MESH)
            copy.start()
            copies.append(copy)
        sends.extend(copies)
        return copies

    def summed(buf, axis):
        n = size[axis]
        out = None
        for source in range(n):
            term = buf[lax.rem(idx[axis] - source + n, n)]
            out = term if out is None else out + term
        return out

    copies = exchange(pbuf, "dp", p_send, p_recv)
    for copy in copies:
        copy.wait_recv()
    left = summed(pbuf, "dp") * (1.0 / ndp)
    lefts = [left[:, :n_local], left[:, n_local:]]

    grams = [lax.dot_general(x, x, (((1,), (1,)), ((), ())), precision=HIGHEST, preferred_element_type=F32)
             for x in lefts]
    for p in range(2):
        gbuf[0, p] = grams[p]
    gram_copies = exchange(gbuf, "tensor", g_send, g_recv)

    pieces = [jnp.concatenate(split3(jnp.concatenate([x, x], axis=1)), axis=0) for x in lefts]

    coords = {}
    for order in plan.orders:
        for axis, stride, n in order:
            coords[axis, stride, n] = lax.rem(idx[axis] // stride, n)

    def peer(stage, coordinate):
        axis, stride, n = stage
        return device(axis, idx[axis] + (coordinate - coords[stage]) * stride)

    def right_term(p, j, h):
        first = h * plan.half + j * plan.sizes[p][0]
        columns = plan.sizes[p][0] * 8 * 128 // rank
        block = min(BLOCK, columns)
        per = rank // 8

        def body(i, _):
            tile = first + i * (block // 128 * per)
            col = pl.multiple_of(tile // per * 128, 128)
            w = jnp.dot(pieces[p], ge[p, :, pl.ds(col, block)], preferred_element_type=F32)
            w = (w[2 * rank:] + w[rank:2 * rank]) + w[:rank]
            for b in range(block // 128):
                part[p, pl.ds(tile + b * per, per)] = w[:, b * 128:(b + 1) * 128].reshape(per, 8, 128)
            return 0

        lax.fori_loop(0, columns // block, body, 0, unroll=True)

    def current(p, s, j, d):
        t = plan.sizes[p][s]
        if s == 0:
            return part.at[p, pl.ds(d * plan.half + j * t, t)]
        return acc[p][s - 1].at[j, pl.ds(d * t, t)]

    def offset(p, s, j, last=None):
        out = coords[plan.core] * plan.half if s or last is None else last * plan.half
        out += j * plan.sizes[p][0]
        for i in range(1, s + 1):
            stage = plan.orders[p][i]
            out += (last if i == s and last is not None else coords[stage]) * plan.sizes[p][i]
        return out

    first_sem = [[sum(n - 1 for _, _, n in plan.orders[p][:s]) for s in range(4)] for p in range(2)]
    waiting = {}

    def scatter_start(p, s, j):
        stage = plan.orders[p][s]
        n = stage[2]
        for o in range(1, n):
            to = lax.rem(coords[stage] + o, n)
            q = first_sem[p][s] + o - 1
            copy = pltpu.make_async_remote_copy(
                src_ref=current(p, s, j, to), dst_ref=recv[p][s].at[j, o - 1],
                send_sem=rs_send.at[p, j, q], recv_sem=rs_recv.at[p, j, q],
                device_id=peer(stage, to), device_id_type=pl.DeviceIdType.MESH)
            copy.start()
            sends.append(copy)
            waiting.setdefault((0, p, s, j), []).append(copy)

    def scatter_finish(p, s, j):
        stage = plan.orders[p][s]
        for copy in waiting[0, p, s, j]:
            copy.wait_recv()
        total = current(p, s, j, coords[stage])[...]
        for o in range(1, stage[2]):
            total = total + recv[p][s][j, o - 1]
        if s < 3:
            acc[p][s][j] = total
        else:
            full[p, pl.ds(offset(p, 3, j), plan.sizes[p][3])] = total

    def gather_start(p, s, j):
        stage = plan.orders[p][s]
        n = stage[2]
        t = plan.sizes[p][s]
        mine = full.at[p, pl.ds(offset(p, s, j), t)]
        for o in range(1, n):
            to = lax.rem(coords[stage] + o, n)
            source = lax.rem(coords[stage] - o + n, n)
            q = first_sem[p][s] + o - 1
            common = dict(send_sem=ag_send.at[p, j, q], recv_sem=ag_recv.at[p, j, q],
                          device_id=peer(stage, to), device_id_type=pl.DeviceIdType.MESH)
            copy = pltpu.make_async_remote_copy(src_ref=mine, dst_ref=mine, **common)
            copy.start()
            sends.append(copy)
            arrival = pltpu.make_async_remote_copy(
                src_ref=mine, dst_ref=full.at[p, pl.ds(offset(p, s, j, source), t)], **common)
            waiting.setdefault((1, p, s, j), []).append(arrival)

    def gather_finish(p, s, j):
        for copy in waiting[1, p, s, j]:
            copy.wait_recv()

    outs = []

    def step(p, j, s):
        core = coords[plan.core]
        if s == 0:
            right_term(p, j, 1 - core)
            scatter_start(p, 0, j)
            right_term(p, j, core)
        elif s <= 4:
            scatter_finish(p, s - 1, j)
            if s < 4:
                scatter_start(p, s, j)
            else:
                gather_start(p, 3, j)
        elif s <= 8:
            gather_finish(p, 8 - s, j)
            if s < 8:
                gather_start(p, 7 - s, j)
            else:
                t = plan.sizes[p][0]
                for h in range(2):
                    span = pl.ds(h * plan.half + j * t, t)
                    copy = pltpu.make_async_copy(full.at[p, span], w_out.at[p, span], out_sem.at[p, j, h])
                    copy.start()
                    outs.append(copy)

    def coefficients():
        for copy in gram_copies:
            copy.wait_recv()
        for p in range(2):
            gram = None
            for source in range(nt):
                term = gbuf[lax.rem(idx["tensor"] - source + nt, nt), p]
                gram = term if gram is None else gram + term
            c = jnp.dot(spd_inverse(gram), lefts[p], precision=HIGHEST, preferred_element_type=F32) * (1.0 / ndp)
            c0, c1, c2 = split3(c)
            cbuf[p] = jnp.concatenate([c0, c0, c0, c1, c1, c2], axis=0)
        copy = pltpu.make_async_copy(cbuf, c_out, out_sem.at[0, 0, 2])
        copy.start()
        outs.append(copy)

    for wave in range(9 + plan.chunks - 1):
        for j in range(plan.chunks):
            for p in range(2):
                if 0 <= wave - j <= 8:
                    step(p, j, wave - j)
        if wave == 2:
            coefficients()

    for copy in sends:
        copy.wait_send()
    for copy in outs:
        copy.wait()


def finish_kernel(rank, w_ref, c_ref, g0, g1, e0, e1, m0, m1, n0, n1):
    per = rank // 8
    width = g0.shape[1]
    for p, (g, e, m, new) in enumerate(((g0, e0, m0, n0), (g1, e1, m1, n1))):
        w = jnp.concatenate(
            [w_ref[p, b * per:(b + 1) * per].reshape(rank, 128) for b in range(width // 128)], axis=1)
        w0, w1, w2 = split3(w)
        w6 = jnp.concatenate([w0, w1, w2, w0, w1, w0], axis=0)
        a = lax.dot_general(c_ref[p], w6, (((0,), (0,)), ((), ())), preferred_element_type=F32)
        m[...] = a.astype(BF16)
        new[...] = (g[...].astype(F32) + e[...].astype(F32) - a).astype(BF16)


def per_device(ndp, nt, gate_grads, up_grads, gate_errors, up_errors, gate_start, up_start):
    grads = (gate_grads[0], up_grads[0])
    errors = (gate_errors[0], up_errors[0])
    starts = (gate_start.T, up_start.T)
    n_local, cols = grads[0].shape
    rank = gate_start.shape[1]
    plan = Plan(ndp, nt, cols, rank)
    dma = pltpu.SemaphoreType.DMA
    tile = (8, 128)
    j = plan.chunks
    scratch = [
        pltpu.VMEM((2, 2 * n_local, cols), BF16),
        pltpu.VMEM((2, rank, cols), F32),
        pltpu.VMEM((ndp, rank, 2 * n_local), F32),
        pltpu.VMEM((nt, 2, rank, rank), F32),
        pltpu.VMEM((2, plan.tiles) + tile, F32),
        pltpu.VMEM((2, plan.tiles) + tile, F32),
        pltpu.VMEM((2, 6 * rank, n_local), BF16),
    ]
    for p in range(2):
        for s in range(4):
            scratch.append(pltpu.VMEM((j, plan.orders[p][s][2] - 1, plan.sizes[p][s]) + tile, F32))
    for p in range(2):
        for s in range(3):
            scratch.append(pltpu.VMEM((j, plan.sizes[p][s]) + tile, F32))
    scratch += [
        dma((2, LOADS, 3)),
        dma((ndp - 1,)), dma((ndp - 1,)), dma((nt - 1,)), dma((nt - 1,)),
        dma((2, j, plan.copies)), dma((2, j, plan.copies)), dma((2, j, plan.copies)), dma((2, j, plan.copies)),
        dma((2, j, 3)),
    ]
    anywhere = pl.BlockSpec(memory_space=pl.ANY)
    w, c = pl.pallas_call(
        functools.partial(kernel, plan, ndp, nt, rank),
        out_shape=(jax.ShapeDtypeStruct((2, plan.tiles) + tile, F32),
                   jax.ShapeDtypeStruct((2, 6 * rank, n_local), BF16)),
        in_specs=[anywhere] * 6,
        out_specs=(anywhere, anywhere),
        scratch_shapes=scratch,
        compiler_params=pltpu.CompilerParams(collective_id=0, has_side_effects=True,
                                             vmem_limit_bytes=32 * 1024 * 1024),
        name="reduce_right",
    )(*grads, *errors, *starts)

    blocks = 4
    width = cols // blocks
    wide = pl.BlockSpec((n_local, width), lambda i: (0, i))
    gate_mean, up_mean, gate_new, up_new = pl.pallas_call(
        functools.partial(finish_kernel, rank),
        grid=(blocks,),
        out_shape=(jax.ShapeDtypeStruct((n_local, cols), BF16),) * 4,
        in_specs=[pl.BlockSpec((2, plan.tiles // blocks) + tile, lambda i: (0, i, 0, 0)),
                  pl.BlockSpec((2, 6 * rank, n_local), lambda i: (0, 0, 0))] + [wide] * 4,
        out_specs=(wide,) * 4,
        compiler_params=pltpu.CompilerParams(vmem_limit_bytes=32 * 1024 * 1024),
        name="form_outputs",
    )(w, c, *grads, *errors)
    return gate_mean, up_mean, gate_new[None], up_new[None]


def solution(mesh):
    rows = P("dp", "tensor", None)
    return jax.shard_map(
        functools.partial(per_device, mesh.shape["dp"], mesh.shape["tensor"]),
        mesh=mesh,
        in_specs=(rows, rows, rows, rows, P(), P()),
        out_specs=(P("tensor", None), P("tensor", None), rows, rows),
        check_vma=False,
    )
```

```python
import functools

import jax
import jax.numpy as jnp
from jax import lax
from jax.experimental import pallas as pl
from jax.experimental.pallas import tpu as pltpu
from jax.sharding import PartitionSpec as P

F32 = jnp.float32
BF16 = jnp.bfloat16
HIGHEST = lax.Precision.HIGHEST
LOADS = 4
CHUNKS = 2
BLOCK = 512


def split3(x):
    a = x.astype(BF16)
    r = x - a.astype(F32)
    b = r.astype(BF16)
    c = (r - b.astype(F32)).astype(BF16)
    return a, b, c


def inverse_steps(a, steps):
    n = a.shape[0]
    rows = lax.broadcasted_iota(jnp.int32, (n, n), 0)
    cols = lax.broadcasted_iota(jnp.int32, (n, n), 1)
    for k in steps:
        row = a[k:k + 1, :]
        col = a[:, k:k + 1]
        inv = 1.0 / row[:, k:k + 1]
        scaled = row * inv
        new = jnp.where(cols == k, -col * inv, a - col * scaled)
        a = jnp.where(rows == k, jnp.where(cols == k, inv, scaled), new)
    return a


class Plan:
    def __init__(self, ndp, nt, cols, rank):
        self.core = ("tensor", 1, 2)
        self.y = ("tensor", 2, nt // 2)
        self.x = ("dp", 1, 2)
        self.z = ("dp", 2, ndp // 2)
        self.orders = ((self.core, self.x, self.y, self.z), (self.core, self.y, self.x, self.z))
        self.tiles = (rank // 8) * (cols // 128)
        self.half = self.tiles // 2
        shards = (ndp * nt) // 2
        self.chunks = max(1, min(CHUNKS, self.half // shards))
        assert self.half % (shards * self.chunks) == 0
        self.sizes = []
        for order in self.orders:
            t = [self.half // self.chunks]
            for _, _, n in order[1:]:
                t.append(t[-1] // n)
            self.sizes.append(t)
        self.stages = 4
        self.copies = sum(n - 1 for _, _, n in self.orders[0])


def kernel(plan, ndp, nt, rank, *refs):
    grads, errors, starts = refs[0:2], refs[2:4], refs[4:6]
    w_out, c_out = refs[6:8]
    (ge, st, pbuf, gbuf, part, full, cbuf) = refs[8:15]
    k = 15
    recv = (refs[k:k + 4], refs[k + 4:k + 8])
    acc = (refs[k + 8:k + 11], refs[k + 11:k + 14])
    k += 14
    (load_sem, p_send, p_recv, g_send, g_recv, rs_send, rs_recv, ag_send, ag_recv, out_sem) = refs[k:]

    idx = {"dp": lax.axis_index("dp"), "tensor": lax.axis_index("tensor")}
    size = {"dp": ndp, "tensor": nt}

    def device(axis, i):
        return (i, idx["tensor"]) if axis == "dp" else (idx["dp"], i)

    barrier = pltpu.get_barrier_semaphore()
    for axis in ("dp", "tensor"):
        for o in range(1, size[axis]):
            pl.semaphore_signal(barrier, inc=1, device_id=device(axis, lax.rem(idx[axis] + o, size[axis])),
                                device_id_type=pl.DeviceIdType.MESH)

    n_local, cols = grads[0].shape
    width = cols // LOADS
    loads = {}
    for p in range(2):
        for b in range(LOADS):
            span = pl.ds(b * width, width)
            trio = (
                (starts[p].at[:, span], st.at[p, :, span]),
                (grads[p].at[:, span], ge.at[p, pl.ds(0, n_local), span]),
                (errors[p].at[:, span], ge.at[p, pl.ds(n_local, n_local), span]),
            )
            for m, (src, dst) in enumerate(trio):
                copy = pltpu.make_async_copy(src, dst, load_sem.at[p, b, m])
                copy.start()
                loads[p, b, m] = copy

    def left_term(p):
        total = jnp.zeros((3 * rank, 2 * n_local), F32)
        for b in range(LOADS):
            for m in range(3):
                loads[p, b, m].wait()
            s3 = jnp.concatenate(split3(st[p, :, b * width:(b + 1) * width]), axis=0)
            total += lax.dot_general(s3, ge[p, :, b * width:(b + 1) * width], (((1,), (1,)), ((), ())),
                                     preferred_element_type=F32)
        t = (total[2 * rank:] + total[rank:2 * rank]) + total[:rank]
        t = t[:, :n_local] + t[:, n_local:]
        pbuf[p, 0] = jnp.concatenate([t[:rank // 2], t[rank // 2:]], axis=1)

    sends = []

    def exchange(buf, axis, send_sem, recv_sem):
        n = size[axis]
        copies = []
        for o in range(1, n):
            copy = pltpu.make_async_remote_copy(
                src_ref=buf.at[0], dst_ref=buf.at[o], send_sem=send_sem.at[o - 1], recv_sem=recv_sem.at[o - 1],
                device_id=device(axis, lax.rem(idx[axis] + o, n)), device_id_type=pl.DeviceIdType.MESH)
            copy.start()
            copies.append(copy)
        sends.extend(copies)
        return copies

    def summed(buf, axis):
        n = size[axis]
        out = None
        for source in range(n):
            term = buf[lax.rem(idx[axis] - source + n, n)]
            out = term if out is None else out + term
        return out

    left_term(0)
    pl.semaphore_wait(barrier, ndp + nt - 2)
    left_copies = [exchange(pbuf.at[0], "dp", p_send.at[0], p_recv.at[0])]
    left_term(1)
    left_copies.append(exchange(pbuf.at[1], "dp", p_send.at[1], p_recv.at[1]))
    lefts, pieces, gram_copies = {}, {}, {}

    def left_finish(p):
        for copy in left_copies[p]:
            copy.wait_recv()
        x = summed(pbuf.at[p], "dp") * (1.0 / ndp)
        x = jnp.concatenate([x[:, :n_local], x[:, n_local:]], axis=0)
        lefts[p] = x
        pieces[p] = jnp.concatenate(split3(jnp.concatenate([x, x], axis=1)), axis=0)

    def gram_start(p):
        x = lefts[p]
        gbuf[p, 0] = lax.dot_general(x, x, (((1,), (1,)), ((), ())), precision=HIGHEST, preferred_element_type=F32)
        gram_copies[p] = exchange(gbuf.at[p], "tensor", g_send.at[p], g_recv.at[p])

    coords = {}
    for order in plan.orders:
        for axis, stride, n in order:
            coords[axis, stride, n] = lax.rem(idx[axis] // stride, n)

    def peer(stage, coordinate):
        axis, stride, n = stage
        return device(axis, idx[axis] + (coordinate - coords[stage]) * stride)

    def right_term(p, j, h):
        first = h * plan.half + j * plan.sizes[p][0]
        columns = plan.sizes[p][0] * 8 * 128 // rank
        block = min(BLOCK, columns)
        per = rank // 8

        def body(i, _):
            tile = first + i * (block // 128 * per)
            col = pl.multiple_of(tile // per * 128, 128)
            w = jnp.dot(pieces[p], ge[p, :, pl.ds(col, block)], preferred_element_type=F32)
            w = (w[2 * rank:] + w[rank:2 * rank]) + w[:rank]
            for b in range(block // 128):
                part[p, pl.ds(tile + b * per, per)] = w[:, b * 128:(b + 1) * 128].reshape(per, 8, 128)
            return 0

        lax.fori_loop(0, columns // block, body, 0, unroll=True)

    def current(p, s, j, d):
        t = plan.sizes[p][s]
        if s == 0:
            return part.at[p, pl.ds(d * plan.half + j * t, t)]
        return acc[p][s - 1].at[j, pl.ds(d * t, t)]

    def offset(p, s, j, last=None):
        out = coords[plan.core] * plan.half if s or last is None else last * plan.half
        out += j * plan.sizes[p][0]
        for i in range(1, s + 1):
            stage = plan.orders[p][i]
            out += (last if i == s and last is not None else coords[stage]) * plan.sizes[p][i]
        return out

    first_sem = [[sum(n - 1 for _, _, n in plan.orders[p][:s]) for s in range(4)] for p in range(2)]
    waiting = {}

    def scatter_start(p, s, j):
        stage = plan.orders[p][s]
        n = stage[2]
        for o in range(1, n):
            to = lax.rem(coords[stage] + o, n)
            q = first_sem[p][s] + o - 1
            copy = pltpu.make_async_remote_copy(
                src_ref=current(p, s, j, to), dst_ref=recv[p][s].at[j, o - 1],
                send_sem=rs_send.at[p, j, q], recv_sem=rs_recv.at[p, j, q],
                device_id=peer(stage, to), device_id_type=pl.DeviceIdType.MESH)
            copy.start()
            sends.append(copy)
            waiting.setdefault((0, p, s, j), []).append(copy)

    def scatter_finish(p, s, j):
        stage = plan.orders[p][s]
        for copy in waiting[0, p, s, j]:
            copy.wait_recv()
        total = current(p, s, j, coords[stage])[...]
        for o in range(1, stage[2]):
            total = total + recv[p][s][j, o - 1]
        if s < 3:
            acc[p][s][j] = total
        else:
            full[p, pl.ds(offset(p, 3, j), plan.sizes[p][3])] = total

    def gather_start(p, s, j):
        stage = plan.orders[p][s]
        n = stage[2]
        t = plan.sizes[p][s]
        mine = full.at[p, pl.ds(offset(p, s, j), t)]
        for o in range(1, n):
            to = lax.rem(coords[stage] + o, n)
            source = lax.rem(coords[stage] - o + n, n)
            q = first_sem[p][s] + o - 1
            common = dict(send_sem=ag_send.at[p, j, q], recv_sem=ag_recv.at[p, j, q],
                          device_id=peer(stage, to), device_id_type=pl.DeviceIdType.MESH)
            copy = pltpu.make_async_remote_copy(src_ref=mine, dst_ref=mine, **common)
            copy.start()
            sends.append(copy)
            arrival = pltpu.make_async_remote_copy(
                src_ref=mine, dst_ref=full.at[p, pl.ds(offset(p, s, j, source), t)], **common)
            waiting.setdefault((1, p, s, j), []).append(arrival)

    def gather_finish(p, s, j):
        for copy in waiting[1, p, s, j]:
            copy.wait_recv()

    outs = []

    def step(p, j, s):
        core = coords[plan.core]
        if s == 0:
            if j == 0:
                left_finish(p)
            right_term(p, j, 1 - core)
            scatter_start(p, 0, j)
            if j == 0:
                gram_start(p)
            right_term(p, j, core)
        elif s <= 4:
            scatter_finish(p, s - 1, j)
            if s < 4:
                scatter_start(p, s, j)
            else:
                gather_start(p, 3, j)
        elif s <= 8:
            gather_finish(p, 8 - s, j)
            if s < 8:
                gather_start(p, 7 - s, j)
            else:
                t = plan.sizes[p][0]
                for h in range(2):
                    span = pl.ds(h * plan.half + j * t, t)
                    copy = pltpu.make_async_copy(full.at[p, span], w_out.at[p, span], out_sem.at[p, j, h])
                    copy.start()
                    outs.append(copy)

    inverses = {}

    def inverse_start(p):
        for copy in gram_copies[p]:
            copy.wait_recv()
        inverses[p] = summed(gbuf.at[p], "tensor")

    def coefficients():
        for p in range(2):
            c = jnp.dot(inverses[p], lefts[p], precision=HIGHEST, preferred_element_type=F32) * (1.0 / ndp)
            c0, c1, c2 = split3(c)
            cbuf[p] = jnp.concatenate([c0, c0, c0, c1, c1, c2], axis=0)
        copy = pltpu.make_async_copy(cbuf, c_out, out_sem.at[0, 0, 2])
        copy.start()
        outs.append(copy)

    per_wave = -(-rank // 7)
    for wave in range(9 + plan.chunks - 1):
        for j in range(plan.chunks):
            for p in range(2):
                if 0 <= wave - j <= 8:
                    step(p, j, wave - j)
        if wave == 2:
            for p in range(2):
                inverse_start(p)
        if 2 <= wave <= 8:
            first = (wave - 2) * per_wave
            for p in range(2):
                inverses[p] = inverse_steps(inverses[p], range(first, min(first + per_wave, rank)))
        if wave == 8:
            coefficients()

    for copy in sends:
        copy.wait_send()
    for copy in outs:
        copy.wait()


def finish_kernel(rank, w_ref, c_ref, g0, g1, e0, e1, m0, m1, n0, n1):
    per = rank // 8
    width = g0.shape[1]
    for p, (g, e, m, new) in enumerate(((g0, e0, m0, n0), (g1, e1, m1, n1))):
        w = jnp.concatenate(
            [w_ref[p, b * per:(b + 1) * per].reshape(rank, 128) for b in range(width // 128)], axis=1)
        w0, w1, w2 = split3(w)
        w6 = jnp.concatenate([w0, w1, w2, w0, w1, w0], axis=0)
        a = lax.dot_general(c_ref[p], w6, (((0,), (0,)), ((), ())), preferred_element_type=F32)
        m[...] = a.astype(BF16)
        new[...] = (g[...].astype(F32) + e[...].astype(F32) - a).astype(BF16)


def per_device(ndp, nt, gate_grads, up_grads, gate_errors, up_errors, gate_start, up_start):
    grads = (gate_grads[0], up_grads[0])
    errors = (gate_errors[0], up_errors[0])
    starts = (gate_start.T, up_start.T)
    n_local, cols = grads[0].shape
    rank = gate_start.shape[1]
    plan = Plan(ndp, nt, cols, rank)
    dma = pltpu.SemaphoreType.DMA
    tile = (8, 128)
    j = plan.chunks
    scratch = [
        pltpu.VMEM((2, 2 * n_local, cols), BF16),
        pltpu.VMEM((2, rank, cols), F32),
        pltpu.VMEM((2, ndp, rank // 2, 2 * n_local), F32),
        pltpu.VMEM((2, nt, rank, rank), F32),
        pltpu.VMEM((2, plan.tiles) + tile, F32),
        pltpu.VMEM((2, plan.tiles) + tile, F32),
        pltpu.VMEM((2, 6 * rank, n_local), BF16),
    ]
    for p in range(2):
        for s in range(4):
            scratch.append(pltpu.VMEM((j, plan.orders[p][s][2] - 1, plan.sizes[p][s]) + tile, F32))
    for p in range(2):
        for s in range(3):
            scratch.append(pltpu.VMEM((j, plan.sizes[p][s]) + tile, F32))
    scratch += [
        dma((2, LOADS, 3)),
        dma((2, ndp - 1)), dma((2, ndp - 1)), dma((2, nt - 1)), dma((2, nt - 1)),
        dma((2, j, plan.copies)), dma((2, j, plan.copies)), dma((2, j, plan.copies)), dma((2, j, plan.copies)),
        dma((2, j, 3)),
    ]
    anywhere = pl.BlockSpec(memory_space=pl.ANY)
    w, c = pl.pallas_call(
        functools.partial(kernel, plan, ndp, nt, rank),
        out_shape=(jax.ShapeDtypeStruct((2, plan.tiles) + tile, F32),
                   jax.ShapeDtypeStruct((2, 6 * rank, n_local), BF16)),
        in_specs=[anywhere] * 6,
        out_specs=(anywhere, anywhere),
        scratch_shapes=scratch,
        compiler_params=pltpu.CompilerParams(collective_id=0, has_side_effects=True,
                                             vmem_limit_bytes=62 * 1024 * 1024),
        name="reduce_right",
    )(*grads, *errors, *starts)

    blocks = 4
    width = cols // blocks
    wide = pl.BlockSpec((n_local, width), lambda i: (0, i))
    gate_mean, up_mean, gate_new, up_new = pl.pallas_call(
        functools.partial(finish_kernel, rank),
        grid=(blocks,),
        out_shape=(jax.ShapeDtypeStruct((n_local, cols), BF16),) * 4,
        in_specs=[pl.BlockSpec((2, plan.tiles // blocks) + tile, lambda i: (0, i, 0, 0)),
                  pl.BlockSpec((2, 6 * rank, n_local), lambda i: (0, 0, 0))] + [wide] * 4,
        out_specs=(wide,) * 4,
        compiler_params=pltpu.CompilerParams(vmem_limit_bytes=62 * 1024 * 1024),
        name="form_outputs",
    )(w, c, *grads, *errors)
    return gate_mean, up_mean, gate_new[None], up_new[None]


def solution(mesh):
    rows = P("dp", "tensor", None)
    return jax.shard_map(
        functools.partial(per_device, mesh.shape["dp"], mesh.shape["tensor"]),
        mesh=mesh,
        in_specs=(rows, rows, rows, rows, P(), P()),
        out_specs=(P("tensor", None), P("tensor", None), rows, rows),
        check_vma=False,
    )
```

```python
import functools

import jax
import jax.numpy as jnp
from jax import lax
from jax.experimental import pallas as pl
from jax.experimental.pallas import tpu as pltpu
from jax.sharding import PartitionSpec as P

F32 = jnp.float32
BF16 = jnp.bfloat16
HIGHEST = lax.Precision.HIGHEST
LOADS = 4
CHUNKS = 2
BLOCK = 512


def split3(x):
    a = x.astype(BF16)
    r = x - a.astype(F32)
    b = r.astype(BF16)
    c = (r - b.astype(F32)).astype(BF16)
    return a, b, c


def inverse_steps(a, steps):
    n = a.shape[0]
    rows = lax.broadcasted_iota(jnp.int32, (n, n), 0)
    cols = lax.broadcasted_iota(jnp.int32, (n, n), 1)
    for k in steps:
        row = a[k:k + 1, :]
        col = a[:, k:k + 1]
        inv = 1.0 / row[:, k:k + 1]
        scaled = row * inv
        new = jnp.where(cols == k, -col * inv, a - col * scaled)
        a = jnp.where(rows == k, jnp.where(cols == k, inv, scaled), new)
    return a


class Plan:
    def __init__(self, ndp, nt, cols, rank):
        self.core = ("tensor", 1, 2)
        self.y = ("tensor", 2, nt // 2)
        self.x = ("dp", 1, 2)
        self.z = ("dp", 2, ndp // 2)
        self.orders = ((self.core, self.x, self.y, self.z), (self.core, self.y, self.x, self.z))
        self.tiles = (rank // 8) * (cols // 128)
        self.half = self.tiles // 2
        shards = (ndp * nt) // 2
        self.chunks = max(1, min(CHUNKS, self.half // shards))
        assert self.half % (shards * self.chunks) == 0
        self.sizes = []
        for order in self.orders:
            t = [self.half // self.chunks]
            for _, _, n in order[1:]:
                t.append(t[-1] // n)
            self.sizes.append(t)
        self.stages = 4
        self.copies = sum(n - 1 for _, _, n in self.orders[0])


def kernel(plan, ndp, nt, rank, *refs):
    grads, errors, starts = refs[0:2], refs[2:4], refs[4:6]
    w_out, c_out = refs[6:8]
    (ge, st, pbuf, gbuf, part, full, cbuf) = refs[8:15]
    k = 15
    recv = (refs[k:k + 4], refs[k + 4:k + 8])
    acc = (refs[k + 8:k + 11], refs[k + 11:k + 14])
    k += 14
    (load_sem, p_send, p_recv, g_send, g_recv, rs_send, rs_recv, ag_send, ag_recv, out_sem) = refs[k:]

    idx = {"dp": lax.axis_index("dp"), "tensor": lax.axis_index("tensor")}
    size = {"dp": ndp, "tensor": nt}

    def device(axis, i):
        return (i, idx["tensor"]) if axis == "dp" else (idx["dp"], i)

    barrier = pltpu.get_barrier_semaphore()
    for axis in ("dp", "tensor"):
        for o in range(1, size[axis]):
            pl.semaphore_signal(barrier, inc=1, device_id=device(axis, lax.rem(idx[axis] + o, size[axis])),
                                device_id_type=pl.DeviceIdType.MESH)

    n_local, cols = grads[0].shape
    width = cols // LOADS
    loads = {}
    for p in range(2):
        for b in range(LOADS):
            span = pl.ds(b * width, width)
            trio = (
                (starts[p].at[:, span], st.at[p, :, span]),
                (grads[p].at[:, span], ge.at[p, pl.ds(0, n_local), span]),
                (errors[p].at[:, span], ge.at[p, pl.ds(n_local, n_local), span]),
            )
            for m, (src, dst) in enumerate(trio):
                copy = pltpu.make_async_copy(src, dst, load_sem.at[p, b, m])
                copy.start()
                loads[p, b, m] = copy

    def left_term(p):
        total = jnp.zeros((3 * rank, 2 * n_local), F32)
        for b in range(LOADS):
            for m in range(3):
                loads[p, b, m].wait()
            s3 = jnp.concatenate(split3(st[p, :, b * width:(b + 1) * width]), axis=0)
            total += lax.dot_general(s3, ge[p, :, b * width:(b + 1) * width], (((1,), (1,)), ((), ())),
                                     preferred_element_type=F32)
        t = (total[2 * rank:] + total[rank:2 * rank]) + total[:rank]
        t = t[:, :n_local] + t[:, n_local:]
        pbuf[p, 0] = jnp.concatenate([t[:rank // 2], t[rank // 2:]], axis=1)

    sends = []

    def exchange(buf, axis, send_sem, recv_sem):
        n = size[axis]
        copies = []
        for o in range(1, n):
            copy = pltpu.make_async_remote_copy(
                src_ref=buf.at[0], dst_ref=buf.at[o], send_sem=send_sem.at[o - 1], recv_sem=recv_sem.at[o - 1],
                device_id=device(axis, lax.rem(idx[axis] + o, n)), device_id_type=pl.DeviceIdType.MESH)
            copy.start()
            copies.append(copy)
        sends.extend(copies)
        return copies

    def summed(buf, axis):
        n = size[axis]
        out = None
        for source in range(n):
            term = buf[lax.rem(idx[axis] - source + n, n)]
            out = term if out is None else out + term
        return out

    left_term(0)
    pl.semaphore_wait(barrier, ndp + nt - 2)
    left_copies = [exchange(pbuf.at[0], "dp", p_send.at[0], p_recv.at[0])]
    left_term(1)
    left_copies.append(exchange(pbuf.at[1], "dp", p_send.at[1], p_recv.at[1]))
    lefts, pieces, gram_copies = {}, {}, {}

    def left_finish(p):
        for copy in left_copies[p]:
            copy.wait_recv()
        x = summed(pbuf.at[p], "dp") * (1.0 / ndp)
        x = jnp.concatenate([x[:, :n_local], x[:, n_local:]], axis=0)
        lefts[p] = x
        pieces[p] = jnp.concatenate(split3(jnp.concatenate([x, x], axis=1)), axis=0)

    def gram_start(p):
        x = lefts[p]
        gbuf[p, 0] = lax.dot_general(x, x, (((1,), (1,)), ((), ())), precision=HIGHEST, preferred_element_type=F32)
        gram_copies[p] = exchange(gbuf.at[p], "tensor", g_send.at[p], g_recv.at[p])

    coords = {}
    for order in plan.orders:
        for axis, stride, n in order:
            coords[axis, stride, n] = lax.rem(idx[axis] // stride, n)

    def peer(stage, coordinate):
        axis, stride, n = stage
        return device(axis, idx[axis] + (coordinate - coords[stage]) * stride)

    def right_term(p, j, h):
        first = h * plan.half + j * plan.sizes[p][0]
        columns = plan.sizes[p][0] * 8 * 128 // rank
        block = min(BLOCK, columns)
        per = rank // 8

        def body(i, _):
            tile = first + i * (block // 128 * per)
            col = pl.multiple_of(tile // per * 128, 128)
            w = jnp.dot(pieces[p], ge[p, :, pl.ds(col, block)], preferred_element_type=F32)
            w = (w[2 * rank:] + w[rank:2 * rank]) + w[:rank]
            for b in range(block // 128):
                part[p, pl.ds(tile + b * per, per)] = w[:, b * 128:(b + 1) * 128].reshape(per, 8, 128)
            return 0

        lax.fori_loop(0, columns // block, body, 0, unroll=True)

    def current(p, s, j, d):
        t = plan.sizes[p][s]
        if s == 0:
            return part.at[p, pl.ds(d * plan.half + j * t, t)]
        return acc[p][s - 1].at[j, pl.ds(d * t, t)]

    def offset(p, s, j, last=None):
        out = coords[plan.core] * plan.half if s or last is None else last * plan.half
        out += j * plan.sizes[p][0]
        for i in range(1, s + 1):
            stage = plan.orders[p][i]
            out += (last if i == s and last is not None else coords[stage]) * plan.sizes[p][i]
        return out

    first_sem = [[sum(n - 1 for _, _, n in plan.orders[p][:s]) for s in range(4)] for p in range(2)]
    waiting = {}

    def scatter_start(p, s, j):
        stage = plan.orders[p][s]
        n = stage[2]
        for o in range(1, n):
            to = lax.rem(coords[stage] + o, n)
            q = first_sem[p][s] + o - 1
            copy = pltpu.make_async_remote_copy(
                src_ref=current(p, s, j, to), dst_ref=recv[p][s].at[j, o - 1],
                send_sem=rs_send.at[p, j, q], recv_sem=rs_recv.at[p, j, q],
                device_id=peer(stage, to), device_id_type=pl.DeviceIdType.MESH)
            copy.start()
            sends.append(copy)
            waiting.setdefault((0, p, s, j), []).append(copy)

    def scatter_finish(p, s, j):
        stage = plan.orders[p][s]
        for copy in waiting[0, p, s, j]:
            copy.wait_recv()
        total = current(p, s, j, coords[stage])[...]
        for o in range(1, stage[2]):
            total = total + recv[p][s][j, o - 1]
        if s < 3:
            acc[p][s][j] = total
        else:
            full[p, pl.ds(offset(p, 3, j), plan.sizes[p][3])] = total

    def gather_start(p, s, j):
        stage = plan.orders[p][s]
        n = stage[2]
        t = plan.sizes[p][s]
        mine = full.at[p, pl.ds(offset(p, s, j), t)]
        for o in range(1, n):
            to = lax.rem(coords[stage] + o, n)
            source = lax.rem(coords[stage] - o + n, n)
            q = first_sem[p][s] + o - 1
            common = dict(send_sem=ag_send.at[p, j, q], recv_sem=ag_recv.at[p, j, q],
                          device_id=peer(stage, to), device_id_type=pl.DeviceIdType.MESH)
            copy = pltpu.make_async_remote_copy(src_ref=mine, dst_ref=mine, **common)
            copy.start()
            sends.append(copy)
            arrival = pltpu.make_async_remote_copy(
                src_ref=mine, dst_ref=full.at[p, pl.ds(offset(p, s, j, source), t)], **common)
            waiting.setdefault((1, p, s, j), []).append(arrival)

    def gather_finish(p, s, j):
        for copy in waiting[1, p, s, j]:
            copy.wait_recv()

    outs = []

    def step(p, j, s):
        core = coords[plan.core]
        if s == 0:
            if j == 0:
                left_finish(p)
            right_term(p, j, 1 - core)
            scatter_start(p, 0, j)
            if j == 0:
                gram_start(p)
            right_term(p, j, core)
        elif s <= 4:
            scatter_finish(p, s - 1, j)
            if s < 4:
                scatter_start(p, s, j)
            else:
                gather_start(p, 3, j)
        elif s <= 8:
            gather_finish(p, 8 - s, j)
            if s < 8:
                gather_start(p, 7 - s, j)
            else:
                t = plan.sizes[p][0]
                for h in range(2):
                    span = pl.ds(h * plan.half + j * t, t)
                    copy = pltpu.make_async_copy(full.at[p, span], w_out.at[p, span], out_sem.at[p, j, h])
                    copy.start()
                    outs.append(copy)

    inverses = {}

    def inverse_start(p):
        for copy in gram_copies[p]:
            copy.wait_recv()
        inverses[p] = summed(gbuf.at[p], "tensor")

    def coefficients():
        for p in range(2):
            c = jnp.dot(inverses[p], lefts[p], precision=HIGHEST, preferred_element_type=F32) * (1.0 / ndp)
            c0, c1, c2 = split3(c)
            cbuf[p] = jnp.concatenate([c0, c0, c0, c1, c1, c2], axis=0)
        copy = pltpu.make_async_copy(cbuf, c_out, out_sem.at[0, 0, 2])
        copy.start()
        outs.append(copy)

    per_wave = -(-rank // 7)
    for wave in range(9 + plan.chunks - 1):
        for j in range(plan.chunks):
            for p in range(2):
                if 0 <= wave - j <= 8:
                    step(p, j, wave - j)
        if wave == 2:
            for p in range(2):
                inverse_start(p)
        if 2 <= wave <= 8:
            first = (wave - 2) * per_wave
            for p in range(2):
                inverses[p] = inverse_steps(inverses[p], range(first, min(first + per_wave, rank)))
        if wave == 8:
            coefficients()

    for copy in sends:
        copy.wait_send()
    for copy in outs:
        copy.wait()


def finish_kernel(rank, w_ref, c_ref, g0, g1, e0, e1, m0, m1, n0, n1):
    per = rank // 8
    width = g0.shape[1]
    for p, (g, e, m, new) in enumerate(((g0, e0, m0, n0), (g1, e1, m1, n1))):
        w = jnp.concatenate(
            [w_ref[p, b * per:(b + 1) * per].reshape(rank, 128) for b in range(width // 128)], axis=1)
        w0, w1, w2 = split3(w)
        w6 = jnp.concatenate([w0, w1, w2, w0, w1, w0], axis=0)
        a = lax.dot_general(c_ref[p], w6, (((0,), (0,)), ((), ())), preferred_element_type=F32)
        m[...] = a.astype(BF16)
        new[...] = (g[...].astype(F32) + e[...].astype(F32) - a).astype(BF16)


def per_device(ndp, nt, gate_grads, up_grads, gate_errors, up_errors, gate_start, up_start):
    grads = (gate_grads[0], up_grads[0])
    errors = (gate_errors[0], up_errors[0])
    starts = (gate_start.T, up_start.T)
    n_local, cols = grads[0].shape
    rank = gate_start.shape[1]
    plan = Plan(ndp, nt, cols, rank)
    dma = pltpu.SemaphoreType.DMA
    tile = (8, 128)
    j = plan.chunks
    scratch = [
        pltpu.VMEM((2, 2 * n_local, cols), BF16),
        pltpu.VMEM((2, rank, cols), F32),
        pltpu.VMEM((2, ndp, rank // 2, 2 * n_local), F32),
        pltpu.VMEM((2, nt, rank, rank), F32),
        pltpu.VMEM((2, plan.tiles) + tile, F32),
        pltpu.VMEM((2, plan.tiles) + tile, F32),
        pltpu.VMEM((2, 6 * rank, n_local), BF16),
    ]
    for p in range(2):
        for s in range(4):
            scratch.append(pltpu.VMEM((j, plan.orders[p][s][2] - 1, plan.sizes[p][s]) + tile, F32))
    for p in range(2):
        for s in range(3):
            scratch.append(pltpu.VMEM((j, plan.sizes[p][s]) + tile, F32))
    scratch += [
        dma((2, LOADS, 3)),
        dma((2, ndp - 1)), dma((2, ndp - 1)), dma((2, nt - 1)), dma((2, nt - 1)),
        dma((2, j, plan.copies)), dma((2, j, plan.copies)), dma((2, j, plan.copies)), dma((2, j, plan.copies)),
        dma((2, j, 3)),
    ]
    anywhere = pl.BlockSpec(memory_space=pl.ANY)
    w, c = pl.pallas_call(
        functools.partial(kernel, plan, ndp, nt, rank),
        out_shape=(jax.ShapeDtypeStruct((2, plan.tiles) + tile, F32),
                   jax.ShapeDtypeStruct((2, 6 * rank, n_local), BF16)),
        in_specs=[anywhere] * 6,
        out_specs=(anywhere, anywhere),
        scratch_shapes=scratch,
        compiler_params=pltpu.CompilerParams(collective_id=0, has_side_effects=True,
                                             vmem_limit_bytes=62 * 1024 * 1024),
        name="reduce_right",
    )(*grads, *errors, *starts)

    blocks = 2
    width = cols // blocks
    wide = pl.BlockSpec((n_local, width), lambda i: (0, i))
    gate_mean, up_mean, gate_new, up_new = pl.pallas_call(
        functools.partial(finish_kernel, rank),
        grid=(blocks,),
        out_shape=(jax.ShapeDtypeStruct((n_local, cols), BF16),) * 4,
        in_specs=[pl.BlockSpec((2, plan.tiles // blocks) + tile, lambda i: (0, i, 0, 0)),
                  pl.BlockSpec((2, 6 * rank, n_local), lambda i: (0, 0, 0))] + [wide] * 4,
        out_specs=(wide,) * 4,
        compiler_params=pltpu.CompilerParams(vmem_limit_bytes=62 * 1024 * 1024),
        name="form_outputs",
    )(w, c, *grads, *errors)
    return gate_mean, up_mean, gate_new[None], up_new[None]


def solution(mesh):
    rows = P("dp", "tensor", None)
    return jax.shard_map(
        functools.partial(per_device, mesh.shape["dp"], mesh.shape["tensor"]),
        mesh=mesh,
        in_specs=(rows, rows, rows, rows, P(), P()),
        out_specs=(P("tensor", None), P("tensor", None), rows, rows),
        check_vma=False,
    )
```
